256 devices in a mesh: layer: 8 (over z_hi, core), fsdp: 32 (over x, z_lo, y).
Axes of the slice: x: 4, y: 4, z: 8 (z_hi: 4, z_lo: 2; z = z_hi * 2 + z_lo), core: 2. Of those that a mesh axis runs over, the one named last changes fastest.
Arguments:
- grads: bfloat16 [16, 2048, 2048], P('layer', 'fsdp'), may hold values from -6 to 6
- left_basis: bfloat16 [16, 2048, 2048], P('layer', 'fsdp'), may hold values from -6 to 6
- right_basis: bfloat16 [16, 2048, 2048], P('layer', 'fsdp'), may hold values from -6 to 6
- left_stat: bfloat16 [16, 2048, 2048], P('layer', 'fsdp'), may hold values from -6 to 6
- right_stat: bfloat16 [16, 2048, 2048], P('layer', 'fsdp'), may hold values from -6 to 6
- first_moment: float32 [16, 2048, 2048], P('layer', None, 'fsdp'), may hold values from -3 to 3
- second_moment: float32 [16, 2048, 2048], P('layer', None, 'fsdp'), may hold values from 0.05 to 1
- refresh_flags: int32 [16, 2, 2048], P('layer'), may hold values 0 or 1
Outputs:
- update: bfloat16 [16, 2048, 2048], P('layer', 'fsdp')
- new_first: float32 [16, 2048, 2048], P('layer', None, 'fsdp')
- new_second: float32 [16, 2048, 2048], P('layer', None, 'fsdp')
- new_left: bfloat16 [16, 2048, 2048], P('layer', 'fsdp')
- new_right: bfloat16 [16, 2048, 2048], P('layer', 'fsdp')
The draws below stay inside these ranges and needn't reach their ends.
All inputs are finite; a program needn't handle non-finite values. No bound on the sum of `refresh_flags` on one device may be relied on, other than what follows from the above.
Results may differ from the reference program's by a relative error of at most 0.008.
Values may be sent and summed in bfloat16 or wider, within the bound.
No kernel may reach another device: no remote copies, remote signals or barrier semaphores. Data moves between devices by JAX's collectives and lax.ppermute only.
A program may use at most 128 MiB of HBM per device.

```python
import math
import jax
import jax.numpy as jnp
from jax import lax

B = 2048
LAYERS = 16


def place_ends(drawn, rng, least, largest):
    longest = drawn.shape.index(max(drawn.shape))
    spots = []
    for shift in (0, 1):
        where = [jax.random.randint(jax.random.fold_in(rng, axis), (), 0, length) for axis, length in enumerate(drawn.shape)]
        where[longest] = (where[longest] + shift) % drawn.shape[longest]
        spots.append(tuple(where))
    return drawn.at[spots[0]].set(least).at[spots[1]].set(largest)


def shard_levels(stream_key, dims, cuts, least, largest):
    def one(position, shards_of):
        steps = jax.random.uniform(jax.random.fold_in(jax.random.fold_in(stream_key, 6), position), (shards_of,), jnp.float32, least / len(cuts), largest / len(cuts))
        return jnp.repeat(jnp.exp(steps), dims[position] // shards_of).reshape((-1,) + (1,) * (len(dims) - position - 1))

    factor_of = one(*cuts[0])
    for cut in cuts[1:]:
        factor_of = factor_of * one(*cut)
    return factor_of


def centred(rng, dims, spread, reach, pieces=(), dtype=jnp.bfloat16):
    entries = spread * jax.random.normal(rng, dims, jnp.float32)
    if pieces:
        entries = entries * shard_levels(rng, dims, pieces, -0.22, 0.18)
    return jnp.clip(entries, -reach, reach).astype(dtype)


def setup_inputs(seed: int = 0) -> dict:
    seeds = jax.random.split(jax.random.key(seed), 9)
    grads = centred(seeds[0], (LAYERS, B, B), 1.0, 6.0, ((0, 8), (1, 32)))
    left_basis = centred(seeds[1], (LAYERS, B, B), 1.0, 6.0, ((0, 8), (1, 32)))
    right_basis = centred(seeds[2], (LAYERS, B, B), 1.0, 6.0, ((0, 8), (1, 32)))
    left_stat = centred(seeds[3], (LAYERS, B, B), 1.0, 6.0, ((0, 8), (1, 32)))
    right_stat = centred(seeds[4], (LAYERS, B, B), 1.0, 6.0, ((0, 8), (1, 32)))
    first_moment = centred(seeds[5], (LAYERS, B, B), 0.3, 3.0, ((0, 8), (2, 32)), jnp.float32)
    second_moment = jnp.clip(jnp.exp(math.log(1.0) - 2.9957323 * jax.random.uniform(seeds[6], (LAYERS, B, B), jnp.float32) ** shard_levels(seeds[6], (LAYERS, B, B), ((0, 8), (2, 32)), -0.2, 0.2)), 0.05, 1.0)
    refresh_flags = place_ends((jax.random.randint(seeds[7], (LAYERS, 2, B), 0, 2) < 1).astype(jnp.int32), jax.random.fold_in(seeds[7], 1), 0, 1)
    return dict(grads=grads, left_basis=left_basis, right_basis=right_basis, left_stat=left_stat, right_stat=right_stat, first_moment=first_moment, second_moment=second_moment, refresh_flags=refresh_flags)


def one_layer(grad, left, right, lstat, rstat, first, second, flags):
    root = math.sqrt(B)
    half = (jnp.dot(grad, right, preferred_element_type=jnp.float32) / root).astype(jnp.bfloat16)
    rotated = lax.dot_general(left, half, (((0,), (0,)), ((), ())), preferred_element_type=jnp.float32) / root
    new_first = 0.9 * first + 0.1 * rotated
    new_second = 0.95 * second + 0.05 * rotated * rotated
    direction = (new_first / (jnp.sqrt(new_second) + 1e-08)).astype(jnp.bfloat16)
    back = (jnp.dot(left, direction, preferred_element_type=jnp.float32) / root).astype(jnp.bfloat16)
    raw = lax.dot_general(back, right, (((1,), (1,)), ((), ())), preferred_element_type=jnp.float32) / root
    power_left = jnp.dot(lstat, left, preferred_element_type=jnp.float32)
    power_right = jnp.dot(rstat, right, preferred_element_type=jnp.float32)
    scale_left = lax.optimization_barrier(jnp.mean(power_left * power_left, axis=0))
    scale_right = lax.optimization_barrier(jnp.mean(power_right * power_right, axis=0))
    new_left = jnp.where(flags[0][None, :] == 1, power_left / jnp.sqrt(scale_left + 1e-06), left.astype(jnp.float32)).astype(jnp.bfloat16)
    new_right = jnp.where(flags[1][None, :] == 1, power_right / jnp.sqrt(scale_right + 1e-06), right.astype(jnp.float32)).astype(jnp.bfloat16)
    return (raw, new_first, new_second, new_left, new_right)

def reference(grads, left_basis, right_basis, left_stat, right_stat, first_moment, second_moment, refresh_flags):
    raws, firsts, seconds, lefts, rights = ([], [], [], [], [])
    for layer in range(LAYERS):
        raw, nf, ns, nl, nr = one_layer(grads[layer], left_basis[layer], right_basis[layer], left_stat[layer], right_stat[layer], first_moment[layer], second_moment[layer], refresh_flags[layer])
        raws.append(raw)
        firsts.append(nf)
        seconds.append(ns)
        lefts.append(nl)
        rights.append(nr)
    total = jnp.float32(0.0)
    for raw in raws:
        total = total + jnp.sum(raw * raw)
    rms = jnp.sqrt(total / (LAYERS * B * B) + 1e-06)
    factor = jnp.minimum(1.0, 0.5 / rms)
    update = jnp.stack([(raw * factor).astype(jnp.bfloat16) for raw in raws])
    return (update, jnp.stack(firsts), jnp.stack(seconds), jnp.stack(lefts), jnp.stack(rights))
```

```python
import functools
import math

import jax
import jax.numpy as jnp
from jax import lax
from jax.experimental import pallas as pl
from jax.experimental.pallas import tpu as pltpu
from jax.sharding import Mesh, PartitionSpec as P

BF = jnp.bfloat16
F32 = jnp.float32
W = 2048
C = 64
X = 512
STEPS = (0, -1, 1, 2)
ROOT = 1.0 / math.sqrt(W)
VMEM = 48 * 1024 * 1024
ANY = pl.BlockSpec(memory_space=pl.ANY)
INV = pl.BlockSpec(memory_space=pltpu.VMEM)
INS = pl.BlockSpec(memory_space=pltpu.SMEM)


def piece_list():
    second = {0: 0, -1: 1, 1: 2}
    out = []
    for dx in STEPS:
        rows = []
        for dy in STEPS:
            j = STEPS.index(dx)
            buf, row = (second[dy], j) if dy != 2 else ((3, j) if j < 2 else (4, j - 2))
            rows.append((buf, row * C, 0, dy))
        for dy in STEPS:
            j = STEPS.index(dy)
            buf, row = (second[dx], j) if dx != 2 else ((3, j) if j < 2 else (4, j - 2))
            rows.append((5 + buf, row * C, 1, dy))
        out.append(rows)
    return out


PIECES = piece_list()


def start_loads(pos, refs, dst, sems):
    x, zl, y = pos[0], pos[1], pos[2]
    groups = []
    for g, (dx, rows) in enumerate(zip(STEPS, PIECES)):
        xoff = pl.multiple_of(jnp.bitwise_and(x + dx + 4, 3) * X, X)
        copies = []
        for n, (buf, row, dz, dy) in enumerate(rows):
            z = jnp.bitwise_and(zl + dz, 1)
            yy = jnp.bitwise_and(y + dy + 4, 3)
            off = pl.multiple_of(xoff + z * (4 * C) + yy * C, C)
            cp = pltpu.make_async_copy(
                refs[buf].at[pl.ds(row, C), :], dst.at[pl.ds(off, C), :], sems.at[g * 8 + n]
            )
            cp.start()
            copies.append(cp)
        groups.append((xoff, copies))
    return groups


def half_kernel(*args):
    pos, g_own, g_rec, s_own, s_rec = args[:5]
    pieces = args[5:15]
    out, power, sums, basis, lhs, acc, sems, sems2 = args[15:]
    groups = start_loads(pos, pieces, basis, sems)
    zl = pos[1]
    zo = pl.multiple_of(zl * C, C)
    zr = pl.multiple_of((1 - zl) * C, C)
    lhs[pl.ds(zo, C), :] = g_own[...]
    lhs[pl.ds(zr, C), :] = g_rec[...]
    lhs[pl.ds(2 * C + zo, C), :] = s_own[...]
    lhs[pl.ds(2 * C + zr, C), :] = s_rec[...]
    for i, (xoff, copies) in enumerate(groups):
        for cp in copies:
            cp.wait()

        @pl.loop(0, W // X)
        def _(n):
            no = pl.multiple_of(n * X, X)
            part = jnp.dot(
                lhs[:, pl.ds(xoff, X)], basis[pl.ds(xoff, X), pl.ds(no, X)], preferred_element_type=F32
            )
            if i == 0:
                acc[:, pl.ds(no, X)] = part
            else:
                acc[:, pl.ds(no, X)] += part

    low = lax.broadcasted_iota(jnp.int32, (2 * C, 128), 1) < C
    for xx in range(4):
        for p in range(2):
            t0 = acc[: 2 * C, xx * X + p * 128 : xx * X + p * 128 + 128] * ROOT
            t1 = acc[: 2 * C, xx * X + 256 + p * 128 : xx * X + 256 + p * 128 + 128] * ROOT
            out[xx * 4 + 2 * p] = jnp.where(low, t0, pltpu.roll(t1, C, 1)).astype(BF)
            out[xx * 4 + 2 * p + 1] = jnp.where(low, pltpu.roll(t0, C, 1), t1).astype(BF)
    pw = acc[2 * C :, :]
    power[...] = pw
    sums[...] = jnp.sum(pw * pw, axis=0, keepdims=True)


def left_kernel(*args):
    pos, s_own, s_rec, hcols, m1, m2, sums_r = args[:7]
    pieces = args[7:17]
    out, power, first, second, rot_out, basis, lhs, acc, dire, norm, sems = args[17:]
    groups = start_loads(pos, pieces, basis, sems)
    zl = pos[1]
    zo = pl.multiple_of(zl * C, C)
    zr = pl.multiple_of((1 - zl) * C, C)
    for xx in range(4):
        for z in range(2):
            for p in range(2):
                a = hcols[xx * 4 + 2 * p, z * C : (z + 1) * C, :]
                b = hcols[xx * 4 + 2 * p + 1, z * C : (z + 1) * C, :]
                t = jnp.concatenate([a, b], axis=0).astype(F32)
                lo = xx * X + z * 256 + p * 128
                lhs[: 2 * C, lo : lo + 128] = t.T.astype(BF)
    lhs[pl.ds(2 * C + zo, C), :] = s_own[...]
    lhs[pl.ds(2 * C + zr, C), :] = s_rec[...]
    for i, (xoff, copies) in enumerate(groups):
        for cp in copies:
            cp.wait()

        @pl.loop(0, W // X)
        def _(n):
            no = pl.multiple_of(n * X, X)
            part = jnp.dot(
                lhs[:, pl.ds(xoff, X)], basis[pl.ds(xoff, X), pl.ds(no, X)], preferred_element_type=F32
            )
            if i == 0:
                acc[:, pl.ds(no, X)] = part
            else:
                acc[:, pl.ds(no, X)] += part

    @pl.loop(0, W // 256)
    def _(n):
        no = pl.multiple_of(n * 256, 256)
        rot = acc[: 2 * C, pl.ds(no, 256)].T * ROOT
        nf = 0.9 * m1[pl.ds(no, 256), :] + 0.1 * rot
        ns = 0.95 * m2[pl.ds(no, 256), :] + 0.05 * rot * rot
        first[pl.ds(no, 256), :] = nf
        second[pl.ds(no, 256), :] = ns
        rot_out[pl.ds(no, 256), :] = rot.astype(BF)
        dire[pl.ds(no, 256), :] = (nf / (jnp.sqrt(ns) + 1e-8)).astype(BF)

    pw = acc[2 * C :, :]
    power[...] = pw
    sums_l = jnp.sum(pw * pw, axis=0, keepdims=True)
    for i in range(16):
        norm[i : i + 1, :] = sums_l[:, i * 128 : i * 128 + 128]
        norm[16 + i : 17 + i, :] = sums_r[:, i * 128 : i * 128 + 128]
    nb = norm[...].astype(BF)
    for i in range(16):
        out[i, 2 * C :, :] = nb

    @pl.loop(0, 4)
    def _(xx):
        for z in range(2):
            ro = pl.multiple_of(xx * X + z * 256, 256)
            bk = (jnp.dot(basis[pl.ds(ro, 256), :], dire[...], preferred_element_type=F32) * ROOT).astype(BF)
            for yy in range(4):
                out[xx * 4 + yy, z * C : (z + 1) * C, :] = bk[yy * C : (yy + 1) * C, :]


def raw_kernel(*args):
    pos, brows = args[:2]
    pieces = args[2:12]
    raw, total, basis, lhs, sems = args[12:]
    groups = start_loads(pos, pieces, basis, sems)
    low = lax.broadcasted_iota(jnp.int32, (2 * C, 128), 1) < C
    for xx in range(4):
        for p in range(2):
            b0 = brows[xx * 4 + 2 * p, : 2 * C, :].astype(F32)
            b1 = brows[xx * 4 + 2 * p + 1, : 2 * C, :].astype(F32)
            lo = xx * X + p * 128
            lhs[:, lo : lo + 128] = jnp.where(low, b0, pltpu.roll(b1, C, 1)).astype(BF)
            lhs[:, lo + 256 : lo + 384] = jnp.where(low, pltpu.roll(b0, C, 1), b1).astype(BF)
    tot = jnp.zeros((1, X), F32)
    for xoff, copies in groups:
        for cp in copies:
            cp.wait()
        r = lax.dot_general(
            lhs[...], basis[pl.ds(xoff, X), :], (((1,), (1,)), ((), ())), preferred_element_type=F32
        ) * ROOT
        tot = tot + jnp.sum(r * r, axis=0, keepdims=True)
        raw[:, pl.ds(xoff, X)] = r.astype(BF)
    total[...] = jnp.broadcast_to(jnp.sum(tot, axis=1, keepdims=True), (8, 128))


def params():
    return pltpu.CompilerParams(vmem_limit_bytes=VMEM)


def sds(shape, dtype):
    return jax.ShapeDtypeStruct(shape, dtype)


def call_half(pos, g_own, g_rec, s_own, s_rec, pieces):
    return pl.pallas_call(
        half_kernel,
        out_shape=(sds((16, 2 * C, 128), BF), sds((2 * C, W), F32), sds((1, W), F32)),
        in_specs=[INS] + [INV] * 4 + [ANY] * 10,
        out_specs=(INV,) * 3,
        scratch_shapes=[
            pltpu.VMEM((W, W), BF),
            pltpu.VMEM((4 * C, W), BF),
            pltpu.VMEM((4 * C, W), F32),
            pltpu.SemaphoreType.DMA((32,)),
            pltpu.SemaphoreType.DMA((1,)),
        ],
        compiler_params=params(),
        cost_estimate=pl.CostEstimate(flops=2 * 4 * C * W * W, bytes_accessed=2 * W * W, transcendentals=0),
        name="half",
    )(pos, g_own, g_rec, s_own, s_rec, *pieces)


def call_left(pos, s_own, s_rec, hcols, m1, m2, sums_r, pieces):
    return pl.pallas_call(
        left_kernel,
        out_shape=(
            sds((16, 2 * C + 32, 128), BF),
            sds((2 * C, W), F32),
            sds((W, 128), F32),
            sds((W, 128), F32),
            sds((W, 128), BF),
        ),
        in_specs=[INS] + [INV] * 6 + [ANY] * 10,
        out_specs=(INV,) * 5,
        scratch_shapes=[
            pltpu.VMEM((W, W), BF),
            pltpu.VMEM((4 * C, W), BF),
            pltpu.VMEM((4 * C, W), F32),
            pltpu.VMEM((W, 128), BF),
            pltpu.VMEM((32, 128), F32),
            pltpu.SemaphoreType.DMA((32,)),
        ],
        compiler_params=params(),
        cost_estimate=pl.CostEstimate(flops=2 * 6 * C * W * W, bytes_accessed=2 * W * W, transcendentals=0),
        name="left",
    )(pos, s_own, s_rec, hcols, m1, m2, sums_r, *pieces)


def call_raw(pos, brows, pieces):
    return pl.pallas_call(
        raw_kernel,
        out_shape=(sds((2 * C, W), BF), sds((8, 128), F32)),
        in_specs=[INS, INV] + [ANY] * 10,
        out_specs=(INV,) * 2,
        scratch_shapes=[
            pltpu.VMEM((W, W), BF),
            pltpu.VMEM((2 * C, W), BF),
            pltpu.SemaphoreType.DMA((32,)),
        ],
        compiler_params=params(),
        cost_estimate=pl.CostEstimate(flops=2 * 2 * C * W * W, bytes_accessed=2 * W * W, transcendentals=0),
        name="raw",
    )(pos, brows, *pieces)


def shift(v, axis, by):
    return lax.ppermute(v, axis, [(i, (i + by) % 4) for i in range(4)])


def gather_two(piece, a, b):
    near = [piece, shift(piece, a, 1), shift(piece, a, -1), shift(piece, a, 2)]
    mine = jnp.concatenate(near, axis=0)
    left = shift(mine, b, 1)
    right = shift(mine, b, -1)
    far0 = shift(left[: 2 * C], b, 1)
    far1 = shift(right[2 * C :], b, -1)
    return [mine, left, right, far0, far1]


def swap(v):
    return lax.ppermute(v, "zl", [(0, 1), (1, 0)])


def body(grads, left_basis, right_basis, left_stat, right_stat, first_moment, second_moment, refresh_flags):
    x, zl, y = lax.axis_index("x"), lax.axis_index("zl"), lax.axis_index("y")
    pos = jnp.stack([x, zl, y]).astype(jnp.int32)
    even = zl == 0

    def own(a):
        return lax.dynamic_index_in_dim(a, zl, 0, keepdims=False)

    def oth(a):
        return lax.dynamic_index_in_dim(a, 1 - zl, 0, keepdims=False)

    def both(mine, theirs):
        return jnp.where(even, jnp.stack([mine, theirs]), jnp.stack([theirs, mine]))

    r_own, l_own = own(right_basis), own(left_basis)
    r_rec = swap(oth(right_basis))
    l_rec = swap(oth(left_basis))
    misc = swap(jnp.concatenate([oth(grads), oth(right_stat), oth(left_stat)], axis=0))
    g_rec, sr_rec, sl_rec = misc[:C], misc[C : 2 * C], misc[2 * C :]
    m_rec = swap(jnp.concatenate([oth(first_moment), oth(second_moment)], axis=1).astype(BF)).astype(F32)

    r_pieces = gather_two(r_own, "x", "y") + gather_two(r_rec, "y", "x")
    l_pieces = gather_two(l_own, "x", "y") + gather_two(l_rec, "y", "x")

    half, power_r, sums_r = call_half(pos, own(grads), g_rec, own(right_stat), sr_rec, r_pieces)
    hcols = lax.all_to_all(half, ("x", "y"), split_axis=0, concat_axis=0, tiled=True)

    def wide(mine, theirs):
        return jnp.where(
            even, jnp.concatenate([mine, theirs], axis=1), jnp.concatenate([theirs, mine], axis=1)
        )

    m1 = wide(own(first_moment), m_rec[:, :C])
    m2 = wide(own(second_moment), m_rec[:, C:])
    back, power_l, first, second, rot = call_left(
        pos, own(left_stat), sl_rec, hcols, m1, m2, sums_r, l_pieces
    )
    brows = lax.all_to_all(back, ("x", "y"), split_axis=0, concat_axis=0, tiled=True)
    raw, total = call_raw(pos, brows, r_pieces)

    totals = lax.all_to_all(
        jnp.broadcast_to(total[:1], (256, 128)),
        ("zh", "c", "x", "zl", "y"),
        split_axis=0,
        concat_axis=0,
        tiled=True,
    )
    count = lax.axis_size(("zh", "c")) * 2 * W * W
    rms = jnp.sqrt(jnp.sum(totals[:, 0]) / count + 1e-06)
    factor = jnp.minimum(1.0, 0.5 / rms)

    def rows_own(a):
        return lax.dynamic_slice_in_dim(a, zl * C, C, 0)

    def rows_oth(a):
        return lax.dynamic_slice_in_dim(a, (1 - zl) * C, C, 0)

    raw_rec = swap(rows_oth(raw))
    update = (both(rows_own(raw), raw_rec).astype(F32) * factor).astype(BF)

    cols_own = jnp.where(even, rot[:, :C], rot[:, C:])
    cols_oth = jnp.where(even, rot[:, C:], rot[:, :C])
    rot_rec = swap(cols_oth).astype(F32)
    first_own = jnp.where(even, first[:, :C], first[:, C:])
    second_own = jnp.where(even, second[:, :C], second[:, C:])
    first_rec = 0.9 * oth(first_moment) + 0.1 * rot_rec
    second_rec = 0.95 * oth(second_moment) + 0.05 * rot_rec * rot_rec
    new_first = both(first_own, first_rec)
    new_second = both(second_own, second_rec)

    sums = jnp.sum(brows[:, 2 * C :, :].astype(F32), axis=0).reshape(2, W) / W
    scale = 1.0 / jnp.sqrt(sums + 1e-06)
    flags = own(refresh_flags) == 1

    def refreshed(power, side, rows, basis):
        return jnp.where(flags[side][None], rows(power) * scale[side][None], basis.astype(F32)).astype(BF)

    new_left_own = refreshed(power_l, 0, rows_own, l_own)
    new_right_own = refreshed(power_r, 1, rows_own, r_own)
    ship = swap(
        jnp.concatenate(
            [refreshed(power_l, 0, rows_oth, l_rec), refreshed(power_r, 1, rows_oth, r_rec)], axis=0
        )
    )
    new_left = both(new_left_own, ship[:C])
    new_right = both(new_right_own, ship[C:])
    return update, new_first, new_second, new_left, new_right


def solution(mesh):
    fine = Mesh(mesh.devices.reshape(4, 2, 4, 2, 4), ("zh", "c", "x", "zl", "y"))
    layer, fsdp = ("zh", "c"), ("x", "zl", "y")
    rows, cols = P(layer, fsdp, None), P(layer, None, fsdp)
    return jax.shard_map(
        body,
        mesh=fine,
        in_specs=(rows,) * 5 + (cols,) * 2 + (P(layer, None, None),),
        out_specs=(rows, cols, cols, rows, rows),
        check_vma=False,
    )
```

```python
import math

import jax
import jax.numpy as jnp
from jax import lax
from jax.experimental import pallas as pl
from jax.experimental.pallas import tpu as pltpu
from jax.sharding import Mesh, PartitionSpec as P

BF = jnp.bfloat16
F32 = jnp.float32
W = 2048
C = 64
R = 128
X = 512
STEPS = (0, -1, 1, 2)
ROOT = 1.0 / math.sqrt(W)
VMEM = 48 * 1024 * 1024
NB = 14
ANY = pl.BlockSpec(memory_space=pl.ANY)
INV = pl.BlockSpec(memory_space=pltpu.VMEM)
INS = pl.BlockSpec(memory_space=pltpu.SMEM)


def piece_list():
    out = []
    for dx in STEPS:
        rows = []
        j = STEPS.index(dx)
        for dc in range(2):
            for dz in range(2):
                if dx == 2:
                    rows.append((7 * dc + 3 + dz, 0, dz, 0, dc))
                else:
                    rows.append((7 * dc + j, dz * C, dz, 0, dc))
                rows.append((7 * dc + 5 + dz, j * C, dz, 1, dc))
        out.append(rows)
    return out


PIECES = piece_list()


def start_loads(pos, refs, dst, sems):
    c, x, zl, y = pos[0], pos[1], pos[2], pos[3]
    odd = jnp.bitwise_and(y, 1)
    groups = []
    for g, (dx, rows) in enumerate(zip(STEPS, PIECES)):
        xoff = pl.multiple_of(jnp.bitwise_and(x + dx + 4, 3) * X, X)
        copies = []
        for n, (buf, row, dz, which, dc) in enumerate(rows):
            z = jnp.bitwise_and(zl + dz, 1)
            cc = jnp.bitwise_and(c + dc, 1)
            b = odd if which == 0 else 1 - odd
            off = pl.multiple_of(xoff + z * (4 * C) + cc * R + b * C, C)
            cp = pltpu.make_async_copy(
                refs[buf].at[pl.ds(row, C), :], dst.at[pl.ds(off, C), :], sems.at[g * 8 + n]
            )
            cp.start()
            copies.append(cp)
        groups.append((xoff, copies))
    return groups


def offsets(pos):
    odd = jnp.bitwise_and(pos[3], 1)
    return pl.multiple_of(odd * C, C), pl.multiple_of((1 - odd) * C, C)


def multiply(groups, lhs, basis, acc):
    for i, (xoff, copies) in enumerate(groups):
        for cp in copies:
            cp.wait()

        @pl.loop(0, W // X)
        def _(n):
            no = pl.multiple_of(n * X, X)
            part = jnp.dot(
                lhs[:, pl.ds(xoff, X)], basis[pl.ds(xoff, X), pl.ds(no, X)], preferred_element_type=F32
            )
            if i == 0:
                acc[:, pl.ds(no, X)] = part
            else:
                acc[:, pl.ds(no, X)] += part


def pack_sums(power, norm, out):
    sums = jnp.sum(power * power, axis=0, keepdims=True)
    for i in range(16):
        norm[i : i + 1, :] = sums[:, i * 128 : i * 128 + 128]
    nb = norm[...].astype(BF)
    for i in range(16):
        out[i, R:, :] = nb


def half_kernel(*args):
    pos, gs0, gs1 = args[:3]
    pieces = args[3 : 3 + NB]
    out, power0, power1, basis, lhs, acc, norm, sems = args[3 + NB :]
    groups = start_loads(pos, pieces, basis, sems)
    o0, o1 = offsets(pos)
    lhs[pl.ds(o0, C), :] = gs0[:C, :]
    lhs[pl.ds(o1, C), :] = gs1[:C, :]
    lhs[pl.ds(R + o0, C), :] = gs0[C:, :]
    lhs[pl.ds(R + o1, C), :] = gs1[C:, :]
    multiply(groups, lhs, basis, acc)
    for i in range(16):
        out[i, :R, :] = (acc[:R, i * R : (i + 1) * R] * ROOT).astype(BF)
    power0[...] = acc[pl.ds(R + o0, C), :]
    power1[...] = acc[pl.ds(R + o1, C), :]
    pack_sums(acc[R:, :], norm, out)


def left_kernel(*args):
    pos, s0, s1, hcols, m0, m1 = args[:6]
    pieces = args[6 : 6 + NB]
    out, power0, power1, rot0, rot1, basis, lhs, acc, dire, norm, sems = args[6 + NB :]
    groups = start_loads(pos, pieces, basis, sems)
    o0, o1 = offsets(pos)
    for i in range(16):
        lhs[:R, i * R : (i + 1) * R] = hcols[i, :R, :].astype(F32).T.astype(BF)
    lhs[pl.ds(R + o0, C), :] = s0[...]
    lhs[pl.ds(R + o1, C), :] = s1[...]
    multiply(groups, lhs, basis, acc)
    low = lax.broadcasted_iota(jnp.int32, (256, R), 1) < C
    even = jnp.bitwise_and(pos[3], 1) == 0

    @pl.loop(0, W // 256)
    def _(n):
        no = pl.multiple_of(n * 256, 256)
        rot = acc[:R, pl.ds(no, 256)].T * ROOT
        a = m0[pl.ds(no, 256), :].astype(F32)
        b = m1[pl.ds(no, 256), :].astype(F32)
        a, b = jnp.where(even, a, b), jnp.where(even, b, a)
        first = jnp.where(low, a, pltpu.roll(b, C, 1))
        second = jnp.where(low, pltpu.roll(a, C, 1), b)
        nf = 0.9 * first + 0.1 * rot
        ns = 0.95 * second + 0.05 * rot * rot
        dire[pl.ds(no, 256), :] = (nf / (jnp.sqrt(ns) + 1e-8)).astype(BF)

    rot0[...] = (acc[pl.ds(o0, C), :] * ROOT).astype(BF)
    rot1[...] = (acc[pl.ds(o1, C), :] * ROOT).astype(BF)
    power0[...] = acc[pl.ds(R + o0, C), :]
    power1[...] = acc[pl.ds(R + o1, C), :]
    pack_sums(acc[R:, :], norm, out)

    @pl.loop(0, 8)
    def _(n):
        ro = pl.multiple_of(n * 256, 256)
        bk = (jnp.dot(basis[pl.ds(ro, 256), :], dire[...], preferred_element_type=F32) * ROOT).astype(BF)
        out[2 * n, :R, :] = bk[:R]
        out[2 * n + 1, :R, :] = bk[R:]


def raw_kernel(*args):
    pos, brows = args[:2]
    pieces = args[2 : 2 + NB]
    raw0, raw1, total, basis, lhs, raw, sems = args[2 + NB :]
    groups = start_loads(pos, pieces, basis, sems)
    for i in range(16):
        lhs[:, i * R : (i + 1) * R] = brows[i, :R, :]
    tot = jnp.zeros((1, X), F32)
    for xoff, copies in groups:
        for cp in copies:
            cp.wait()
        r = lax.dot_general(
            lhs[...], basis[pl.ds(xoff, X), :], (((1,), (1,)), ((), ())), preferred_element_type=F32
        ) * ROOT
        tot = tot + jnp.sum(r * r, axis=0, keepdims=True)
        raw[:, pl.ds(xoff, X)] = r.astype(BF)
    o0, o1 = offsets(pos)
    raw0[...] = raw[pl.ds(o0, C), :]
    raw1[...] = raw[pl.ds(o1, C), :]
    total[...] = jnp.broadcast_to(jnp.sum(tot, axis=1, keepdims=True), (256, 128))


def sds(shape, dtype):
    return jax.ShapeDtypeStruct(shape, dtype)


def call(kernel, name, n_vmem, outs, scratch, flops, args, pieces):
    return pl.pallas_call(
        kernel,
        out_shape=outs,
        in_specs=[INS] + [INV] * n_vmem + [ANY] * NB,
        out_specs=(INV,) * len(outs),
        scratch_shapes=scratch + [pltpu.SemaphoreType.DMA((32,))],
        compiler_params=pltpu.CompilerParams(vmem_limit_bytes=VMEM),
        cost_estimate=pl.CostEstimate(flops=flops, bytes_accessed=3 * W * W, transcendentals=0),
        name=name,
    )(*args, *pieces)


BASIS = pltpu.VMEM((W, W), BF)
ROWS32 = sds((C, W), F32)
ROWS16 = sds((C, W), BF)
BLOCKS = sds((16, R + 16, R), BF)


def call_half(pos, gs, pieces):
    scratch = [BASIS, pltpu.VMEM((2 * R, W), BF), pltpu.VMEM((2 * R, W), F32), pltpu.VMEM((16, 128), F32)]
    return call(
        half_kernel, "half", 2, (BLOCKS, ROWS32, ROWS32), scratch, 4 * R * W * W, (pos, *gs), pieces
    )


def call_left(pos, stats, hcols, moments, pieces):
    scratch = [
        BASIS,
        pltpu.VMEM((2 * R, W), BF),
        pltpu.VMEM((2 * R, W), F32),
        pltpu.VMEM((W, R), BF),
        pltpu.VMEM((16, 128), F32),
    ]
    outs = (BLOCKS, ROWS32, ROWS32, ROWS16, ROWS16)
    return call(
        left_kernel, "left", 5, outs, scratch, 6 * R * W * W, (pos, *stats, hcols, *moments), pieces
    )


def call_raw(pos, brows, pieces):
    scratch = [BASIS, pltpu.VMEM((R, W), BF), pltpu.VMEM((R, W), BF)]
    outs = (ROWS16, ROWS16, sds((256, 128), F32))
    return call(raw_kernel, "raw", 1, outs, scratch, 2 * R * W * W, (pos, brows), pieces)


def shift(v, by):
    return lax.ppermute(v, "x", [(i, (i + by) % 4) for i in range(4)])


def swap(v, axis):
    return lax.ppermute(v, axis, [(0, 1), (1, 0)])


def route(k):
    return [(c * 4 + 2 * h + b, h * 4 + 2 * c + (k ^ b)) for c in range(2) for h in range(2) for b in range(2)]


def there(v, k):
    return lax.ppermute(v, ("c", "y"), route(k))


def home(v, k):
    return lax.ppermute(v, ("c", "y"), [(b, a) for a, b in route(k)])


def after(v, *others):
    return lax.optimization_barrier((v,) + others)[0]


def near(u, v):
    mine_u = jnp.concatenate([u, swap(u, "zl")], axis=0)
    mine_v = jnp.concatenate([v, shift(v, 1), shift(v, -1), shift(v, 2)], axis=0)
    return mine_u, mine_v


def further(mine_u, mine_v):
    left, right = shift(mine_u, 1), shift(mine_u, -1)
    return left, right, swap(mine_v, "zl")


def last(left, right):
    return shift(left[:C], 1), shift(right[C:], -1)


def buffers(mine_u, mine_v, left, right, other_v, far0, far1):
    own = [mine_u, left, right, far0, far1, mine_v, other_v]
    return own + [swap(v, "c") for v in own]


def body(grads, left_basis, right_basis, left_stat, right_stat, first_moment, second_moment, refresh_flags):
    c, x, zl, y = (lax.axis_index(a) for a in ("c", "x", "zl", "y"))
    pos = jnp.stack([c, x, zl, y]).astype(jnp.int32)
    odd = jnp.bitwise_and(y, 1)
    even = odd == 0

    def pick(a, k):
        return lax.dynamic_index_in_dim(a, jnp.bitwise_xor(odd, k), 0, keepdims=False)

    def send(*arrays):
        return [there(jnp.concatenate([pick(a, k) for a in arrays], axis=0), k) for k in range(2)]

    def collect(v0, v1):
        return jnp.where(even, jnp.stack([v0, v1]), jnp.stack([v1, v0]))

    r = send(right_basis)
    l = send(after(left_basis, *r))
    gs = send(after(grads, *r), right_stat)
    sl = send(after(left_stat, *l))
    moments = [
        there(
            after(jnp.concatenate([pick(first_moment, k), pick(second_moment, k)], axis=1).astype(BF), *l), k
        )
        for k in range(2)
    ]
    flags = (refresh_flags == 1).astype(BF)
    flags = jnp.where(c == y // 2, flags, swap(flags, "c"))
    flags = pick(flags, 0) == 1

    ru, rv = near(*r)
    lu, lv = near(after(l[0], ru, rv), after(l[1], ru, rv))
    r_left, r_right, r_other = further(ru, rv)
    lu, lv = lax.optimization_barrier((lu, lv, r_left, r_right))[:2]
    r_pieces = buffers(ru, rv, r_left, r_right, r_other, *last(r_left, r_right))
    l_left, l_right, l_other = further(lu, lv)
    l_pieces = buffers(lu, lv, l_left, l_right, l_other, *last(l_left, l_right))

    group = ("x", "zl", "c")
    half, pr0, pr1 = call_half(pos, gs, r_pieces)
    hcols = lax.all_to_all(half, group, split_axis=0, concat_axis=0, tiled=True)

    def refreshed(blocks, side, power, basis):
        scale = jnp.sum(blocks[:, R:, :].astype(F32), axis=0).reshape(1, W) / W
        scale = 1.0 / jnp.sqrt(scale + 1e-06)
        return jnp.where(flags[side][None], power * scale, basis.astype(F32)).astype(BF)

    new_right = collect(*[home(refreshed(hcols, 1, p, b), k) for k, (p, b) in enumerate(zip((pr0, pr1), r))])

    back, pl0, pl1, rot0, rot1 = call_left(pos, sl, hcols, moments, l_pieces)
    brows = lax.all_to_all(back, group, split_axis=0, concat_axis=0, tiled=True)
    rot = [home(rot0, 0), home(rot1, 1)]
    raw0, raw1, total = call_raw(pos, brows, r_pieces)

    totals = lax.all_to_all(total, ("zh", "c", "x", "zl", "y"), split_axis=0, concat_axis=0, tiled=True)
    raws = collect(home(raw0, 0), home(raw1, 1))

    blocks, rot[0], rot[1], _ = lax.optimization_barrier((brows, rot[0], rot[1], raw0))
    new_left = collect(*[home(refreshed(blocks, 0, p, b), k) for k, (p, b) in enumerate(zip((pl0, pl1), l))])
    rotated = jnp.swapaxes(collect(*rot), 1, 2).astype(F32)
    new_first = 0.9 * first_moment + 0.1 * rotated
    new_second = 0.95 * second_moment + 0.05 * rotated * rotated

    count = lax.axis_size(("zh", "c")) * 2 * W * W
    rms = jnp.sqrt(jnp.sum(totals[:, 0]) / count + 1e-06)
    factor = jnp.minimum(1.0, 0.5 / rms)
    update = (raws.astype(F32) * factor).astype(BF)
    return update, new_first, new_second, new_left, new_right


def solution(mesh):
    fine = Mesh(mesh.devices.reshape(4, 2, 4, 2, 4), ("zh", "c", "x", "zl", "y"))
    layer, fsdp = ("zh", "c"), ("x", "zl", "y")
    rows, cols = P(layer, fsdp, None), P(layer, None, fsdp)
    return jax.shard_map(
        body,
        mesh=fine,
        in_specs=(rows,) * 5 + (cols,) * 2 + (P(layer, None, None),),
        out_specs=(rows, cols, cols, rows, rows),
        check_vma=False,
    )
```

```python
import math

import jax
import jax.numpy as jnp
from jax import lax
from jax.experimental import pallas as pl
from jax.experimental.pallas import tpu as pltpu
from jax.sharding import Mesh, PartitionSpec as P

BF = jnp.bfloat16
F32 = jnp.float32
W = 2048
C = 64
R = 128
X = 512
ROOT = 1.0 / math.sqrt(W)
VMEM = 56 * 1024 * 1024
HBM = pl.BlockSpec(memory_space=pltpu.HBM)
INV = pl.BlockSpec(memory_space=pltpu.VMEM)
INS = pl.BlockSpec(memory_space=pltpu.SMEM)


def buffer_list():
    out = []
    for v, blocks in ((0, ((0, 0), (0, 1), (-1, 0), (1, 0), (-1, 1), (1, 1), (2, 0), (2, 1))), (1, ((0, 0), (0, 1)))):
        for dx, dz in blocks:
            out.append(([(0, dx, dz, v)], [(C, dx, dz, v)]))
    for dz in range(2):
        out.append(([(0, -1, dz, 1), (2 * C, 1, dz, 1), (4 * C, 2, dz, 1)], [(C, -1, dz, 1), (3 * C, 1, dz, 1), (5 * C, 2, dz, 1)]))
    return out


BUFFERS = buffer_list()
RIGHT, LEFT = 0, 1


def start_loads(pos, side, refs, dst, sems):
    c, x, zl = pos[0], pos[1], pos[2]
    places = offsets(pos)
    groups = []
    n = 0
    for step in (0, -1, 1, 2):
        xoff = pl.multiple_of(jnp.bitwise_and(x + step + 4, 3) * X, X)
        copies = []
        for dc in range(2):
            for buf, parts in enumerate(BUFFERS):
                for row, dx, dz, which in parts[side]:
                    if dx != step:
                        continue
                    z = jnp.bitwise_and(zl + dz, 1)
                    cc = jnp.bitwise_and(c + dc, 1)
                    off = pl.multiple_of(xoff + z * (2 * R) + cc * R + places[which], C)
                    cp = pltpu.make_async_copy(
                        refs[dc * len(BUFFERS) + buf].at[pl.ds(row, C), :],
                        dst.at[pl.ds(off, C), :],
                        sems.at[n],
                    )
                    cp.start()
                    copies.append(cp)
                    n += 1
        groups.append((xoff, copies))
    return groups


def offsets(pos):
    odd = jnp.bitwise_and(pos[3], 1)
    return pl.multiple_of(odd * C, C), pl.multiple_of((1 - odd) * C, C)


def load_rows(pos, refs, parts, dst, sems, first=32):
    copies = []
    for k, off in enumerate(offsets(pos)):
        for part, row in parts:
            cp = pltpu.make_async_copy(
                refs[k].at[pl.ds(part * C, C), :],
                dst.at[pl.ds(pl.multiple_of(row + off, C), C), :],
                sems.at[first + len(copies)],
            )
            cp.start()
            copies.append(cp)
    return copies


def multiply(groups, lhs, basis, acc):
    for i, (xoff, copies) in enumerate(groups):
        for cp in copies:
            cp.wait()

        @pl.loop(0, W // X)
        def _(n):
            no = pl.multiple_of(n * X, X)
            part = jnp.dot(
                lhs[:, pl.ds(xoff, X)], basis[pl.ds(xoff, X), pl.ds(no, X)], preferred_element_type=F32
            )
            if i == 0:
                acc[:, pl.ds(no, X)] = part
            else:
                acc[:, pl.ds(no, X)] += part


def pack_sums(power, norm, out):
    sums = jnp.sum(power * power, axis=0, keepdims=True)
    for i in range(16):
        norm[i : i + 1, :] = sums[:, i * 128 : i * 128 + 128]
    nb = norm[...].astype(BF)
    for i in range(16):
        out[i, R:, :] = nb


def refresh(blocks, power, norm, outs):
    sums = blocks[0, R:, :].astype(F32)
    for i in range(1, 16):
        sums = sums + blocks[i, R:, :].astype(F32)
    norm[...] = 1.0 / jnp.sqrt(sums / W + 1e-06)
    for i in range(16):
        cols = slice(i * R, (i + 1) * R)
        for k, out in enumerate(outs):
            out[C:, cols] = (power[k * C : (k + 1) * C, cols] * norm[i : i + 1, :]).astype(BF)


def store_rows(pos, src, row, refs, sems, first):
    copies = []
    for k, off in enumerate(offsets(pos)):
        cp = pltpu.make_async_copy(src.at[pl.ds(pl.multiple_of(row + off, C), C), :], refs[k], sems.at[first + k])
        cp.start()
        copies.append(cp)
    return copies


def half_kernel(*args):
    pos, gs = args[0], args[1:3]
    out, power, basis, lhs, acc, norm, sems = args[-7:]
    rows = load_rows(pos, gs, ((0, 0), (1, R)), lhs, sems)
    groups = start_loads(pos, RIGHT, args[3:-7], basis, sems)
    for cp in rows:
        cp.wait()
    multiply(groups, lhs, basis, acc)
    stores = store_rows(pos, acc, R, (power.at[:C], power.at[C:]), sems, 40)
    for i in range(16):
        out[i, :R, :] = (acc[:R, i * R : (i + 1) * R] * ROOT).astype(BF)
    pack_sums(acc[R:, :], norm, out)
    for cp in stores:
        cp.wait()


def left_kernel(*args):
    pos, hcols = args[:2]
    gs, power_r = args[2:4], args[4]
    out, home0, home1, power, basis, lhs, acc, mom, dire, norm, right, sems = args[-12:]
    rows = load_rows(pos, gs, ((2, R),), lhs, sems)
    groups = start_loads(pos, LEFT, args[5:-12], basis, sems)
    later = load_rows(pos, gs, ((3, 0), (4, R)), mom, sems, 34)
    later.append(pltpu.make_async_copy(power_r, right, sems.at[42]))
    later[-1].start()
    for i in range(16):
        lhs[:R, i * R : (i + 1) * R] = hcols[i, :R, :].astype(F32).T.astype(BF)
    for cp in rows:
        cp.wait()
    multiply(groups, lhs, basis, acc)
    stores = store_rows(pos, acc, R, (power.at[:C], power.at[C:]), sems, 40)
    for cp in later:
        cp.wait()
    for i in range(16):
        cols = slice(i * R, (i + 1) * R)
        rot = acc[:R, cols] * ROOT
        nf = 0.9 * mom[:R, cols].astype(F32) + 0.1 * rot
        ns = 0.95 * mom[R:, cols].astype(F32) + 0.05 * rot * rot
        dire[cols, :] = (nf / (jnp.sqrt(ns) + 1e-8)).T.astype(BF)

    o0, o1 = offsets(pos)
    home0[:C, :] = (acc[pl.ds(o0, C), :] * ROOT).astype(BF)
    home1[:C, :] = (acc[pl.ds(o1, C), :] * ROOT).astype(BF)
    refresh(hcols, right, norm, (home0, home1))
    pack_sums(acc[R:, :], norm, out)

    @pl.loop(0, 8)
    def _(n):
        ro = pl.multiple_of(n * 256, 256)
        bk = (jnp.dot(basis[pl.ds(ro, 256), :], dire[...], preferred_element_type=F32) * ROOT).astype(BF)
        out[2 * n, :R, :] = bk[:R]
        out[2 * n + 1, :R, :] = bk[R:]

    for cp in stores:
        cp.wait()


def raw_kernel(*args):
    pos, brows, power_l = args[:3]
    home0, home1, total, basis, lhs, raw, left, norm, sems = args[-9:]
    groups = start_loads(pos, RIGHT, args[3:-9], basis, sems)
    power = pltpu.make_async_copy(power_l, left, sems.at[42])
    power.start()
    for i in range(16):
        lhs[:, i * R : (i + 1) * R] = brows[i, :R, :]
    tot = jnp.zeros((1, X), F32)
    for xoff, copies in groups:
        for cp in copies:
            cp.wait()
        r = lax.dot_general(
            lhs[...], basis[pl.ds(xoff, X), :], (((1,), (1,)), ((), ())), preferred_element_type=F32
        ) * ROOT
        tot = tot + jnp.sum(r * r, axis=0, keepdims=True)
        raw[:, pl.ds(xoff, X)] = r.astype(BF)
    o0, o1 = offsets(pos)
    home0[:C, :] = raw[pl.ds(o0, C), :]
    home1[:C, :] = raw[pl.ds(o1, C), :]
    power.wait()
    refresh(brows, left, norm, (home0, home1))
    total[...] = jnp.broadcast_to(jnp.sum(tot, axis=1, keepdims=True), (256, 128))


def sds(shape, dtype):
    return jax.ShapeDtypeStruct(shape, dtype)


def call(kernel, name, outs, in_hbm, scratch, flops, vmem_args, any_args):
    return pl.pallas_call(
        kernel,
        out_shape=outs,
        in_specs=[INS] + [INV] * (len(vmem_args) - 1) + [HBM] * len(any_args),
        out_specs=(INV,) * (len(outs) - in_hbm) + (HBM,) * in_hbm,
        scratch_shapes=scratch,
        compiler_params=pltpu.CompilerParams(vmem_limit_bytes=VMEM),
        cost_estimate=pl.CostEstimate(flops=flops, bytes_accessed=3 * W * W, transcendentals=0),
        name=name,
    )(*vmem_args, *any_args)


BASIS = pltpu.VMEM((W, W), BF)
SEMS = pltpu.SemaphoreType.DMA((43,))
NORM = pltpu.VMEM((16, 128), F32)
POWER = pltpu.VMEM((R, W), F32)
WIDE = pltpu.VMEM((2 * R, W), BF)
HOME = sds((R, W), BF)
BLOCKS = sds((16, R + 16, R), BF)


def call_half(pos, gs, pieces):
    scratch = [BASIS, WIDE, pltpu.VMEM((2 * R, W), F32), NORM, SEMS]
    outs = (BLOCKS, sds((R, W), F32))
    return call(half_kernel, "half", outs, 1, scratch, 4 * R * W * W, (pos,), (*gs, *pieces))


def call_left(pos, gs, hcols, power_r, pieces):
    scratch = [BASIS, WIDE, pltpu.VMEM((2 * R, W), F32), WIDE, pltpu.VMEM((W, R), BF), NORM, POWER, SEMS]
    outs = (BLOCKS, HOME, HOME, sds((R, W), F32))
    hbm_args = (*gs, power_r, *pieces)
    return call(left_kernel, "left", outs, 1, scratch, 6 * R * W * W, (pos, hcols), hbm_args)


def call_raw(pos, brows, power_l, pieces):
    scratch = [BASIS, pltpu.VMEM((R, W), BF), pltpu.VMEM((R, W), BF), POWER, NORM, SEMS]
    outs = (HOME, HOME, sds((256, 128), F32))
    return call(raw_kernel, "raw", outs, 0, scratch, 2 * R * W * W, (pos, brows), (power_l, *pieces))


def shift(v, by):
    return lax.ppermute(v, "x", [(i, (i + by) % 4) for i in range(4)])


def neighbours(block):
    return [shift(block, 1), shift(block, -1)]


def swap(v, axis):
    return lax.ppermute(v, axis, [(0, 1), (1, 0)])


def route(k):
    return [(c * 4 + 2 * h + b, h * 4 + 2 * c + (k ^ b)) for c in range(2) for h in range(2) for b in range(2)]


def there(v, k):
    return lax.ppermute(v, ("c", "y"), route(k))


def home(v, k):
    return lax.ppermute(v, ("c", "y"), [(b, a) for a, b in route(k)])


def after(v, *others):
    return lax.optimization_barrier((v,) + others)[0]


def body(grads, left_basis, right_basis, left_stat, right_stat, first_moment, second_moment, refresh_flags):
    c, x, zl, y = (lax.axis_index(a) for a in ("c", "x", "zl", "y"))
    pos = jnp.stack([c, x, zl, y]).astype(jnp.int32)
    odd = jnp.bitwise_and(y, 1)
    even = odd == 0

    def pick(a, k):
        return lax.dynamic_index_in_dim(a, jnp.bitwise_xor(odd, k), 0, keepdims=False)

    def send(*arrays):
        return [there(jnp.concatenate([pick(a, k) for a in arrays], axis=0), k) for k in range(2)]

    def collect(v0, v1):
        return jnp.where(even, jnp.stack([v0, v1]), jnp.stack([v1, v0]))

    firsts, seconds = (jnp.swapaxes(m, 1, 2) for m in (first_moment, second_moment))
    u, v = send(right_basis, left_basis)
    rest = send(after(grads, u, v), right_stat, left_stat, firsts.astype(BF), seconds.astype(BF))

    v_near = neighbours(v)
    uz = swap(u, "zl")
    u_near = neighbours(u)
    vz = swap(v, "zl")
    v_far = [shift(after(v_near[0][:C], uz), 1), shift(after(v_near[1][C:], uz), -1)]
    uz_near = neighbours(uz)
    v_all = jnp.concatenate([after(v_near[0], *u_near, vz, *rest), v_near[1], *v_far], axis=0)
    v_all_z = swap(v_all, "zl")
    far = [shift(after(u_near[0], *uz_near), 1), shift(after(uz_near[1], u_near[0]), -1)]
    pieces = [u, uz, *u_near, *uz_near, *far, v, vz, v_all, v_all_z]
    pieces = pieces + [swap(p, "c") for p in pieces[:-1]] + [swap(after(v_all_z, *far), "c")]

    group = ("x", "zl", "c")
    half, power_r = call_half(pos, rest, pieces)
    hcols = lax.all_to_all(half, group, split_axis=0, concat_axis=0, tiled=True)
    back, home0, home1, power_l = call_left(pos, rest, hcols, power_r, pieces)
    brows = lax.all_to_all(back, group, split_axis=0, concat_axis=0, tiled=True)
    early = collect(home(home0, 0), home(home1, 1))
    home0, home1, total = call_raw(pos, brows, power_l, pieces)
    totals = lax.all_to_all(total, ("zh", "c", "x", "zl", "y"), split_axis=0, concat_axis=0, tiled=True)
    late = collect(home(home0, 0), home(home1, 1))

    def refreshed(side, sent, basis):
        return jnp.where(refresh_flags[:, side, None, :] == 1, sent[:, C:], basis)

    new_right = refreshed(1, early, right_basis)
    new_left = refreshed(0, late, left_basis)
    rotated = early[:, :C].astype(F32)
    new_first = jnp.swapaxes(0.9 * firsts + 0.1 * rotated, 1, 2)
    new_second = jnp.swapaxes(0.95 * seconds + 0.05 * rotated * rotated, 1, 2)

    totals = after(totals, new_left, new_right, new_first, new_second)
    count = lax.axis_size(("zh", "c")) * 2 * W * W
    rms = jnp.sqrt(jnp.sum(totals[:, 0]) / count + 1e-06)
    factor = jnp.minimum(1.0, 0.5 / rms)
    update = (late[:, :C].astype(F32) * factor).astype(BF)
    return update, new_first, new_second, new_left, new_right


def solution(mesh):
    fine = Mesh(mesh.devices.reshape(4, 2, 4, 2, 4), ("zh", "c", "x", "zl", "y"))
    layer, fsdp = ("zh", "c"), ("x", "zl", "y")
    rows, cols = P(layer, fsdp, None), P(layer, None, fsdp)
    return jax.shard_map(
        body,
        mesh=fine,
        in_specs=(rows,) * 5 + (cols,) * 2 + (P(layer, None, None),),
        out_specs=(rows, cols, cols, rows, rows),
        check_vma=False,
    )
```

```python
import math

import jax
import jax.numpy as jnp
from jax import lax
from jax.experimental import pallas as pl
from jax.experimental.pallas import tpu as pltpu
from jax.sharding import Mesh, PartitionSpec as P

BF = jnp.bfloat16
F32 = jnp.float32
W = 2048
C = 64
R = 128
X = 512
ROOT = 1.0 / math.sqrt(W)
VMEM = 56 * 1024 * 1024
HBM = pl.BlockSpec(memory_space=pltpu.HBM)
INV = pl.BlockSpec(memory_space=pltpu.VMEM)
INS = pl.BlockSpec(memory_space=pltpu.SMEM)


def buffer_list():
    out = []
    for v, blocks in ((0, ((0, 0), (0, 1), (-1, 0), (1, 0), (-1, 1), (1, 1), (2, 0), (2, 1))), (1, ((0, 0), (0, 1)))):
        for dx, dz in blocks:
            out.append(([(0, dx, dz, v)], [(C, dx, dz, v)]))
    for dz in range(2):
        out.append(([(0, -1, dz, 1), (2 * C, 1, dz, 1), (4 * C, 2, dz, 1)], [(C, -1, dz, 1), (3 * C, 1, dz, 1), (5 * C, 2, dz, 1)]))
    return out


BUFFERS = buffer_list()
RIGHT, LEFT = 0, 1


def start_loads(pos, side, refs, dst, sems):
    c, x, zl = pos[0], pos[1], pos[2]
    places = offsets(pos)
    groups = []
    n = 0
    for step in (0, -1, 1, 2):
        xoff = pl.multiple_of(jnp.bitwise_and(x + step + 4, 3) * X, X)
        copies = []
        for dc in range(2):
            for buf, parts in enumerate(BUFFERS):
                for row, dx, dz, which in parts[side]:
                    if dx != step:
                        continue
                    z = jnp.bitwise_and(zl + dz, 1)
                    cc = jnp.bitwise_and(c + dc, 1)
                    off = pl.multiple_of(xoff + z * (2 * R) + cc * R + places[which], C)
                    cp = pltpu.make_async_copy(
                        refs[dc * len(BUFFERS) + buf].at[pl.ds(row, C), :],
                        dst.at[pl.ds(off, C), :],
                        sems.at[n],
                    )
                    cp.start()
                    copies.append(cp)
                    n += 1
        groups.append((xoff, copies))
    return groups


def offsets(pos):
    odd = jnp.bitwise_and(pos[3], 1)
    return pl.multiple_of(odd * C, C), pl.multiple_of((1 - odd) * C, C)


def load_rows(pos, refs, parts, dst, sems, first=32):
    copies = []
    for k, off in enumerate(offsets(pos)):
        for part, row in parts:
            cp = pltpu.make_async_copy(
                refs[k].at[pl.ds(part * C, C), :],
                dst.at[pl.ds(pl.multiple_of(row + off, C), C), :],
                sems.at[first + len(copies)],
            )
            cp.start()
            copies.append(cp)
    return copies


def multiply(groups, lhs, basis, acc):
    for i, (xoff, copies) in enumerate(groups):
        for cp in copies:
            cp.wait()

        part = jnp.dot(lhs[:, pl.ds(xoff, X)], basis[pl.ds(xoff, X), :], preferred_element_type=F32)
        if i == 0:
            acc[...] = part
        else:
            acc[...] += part


def pack_sums(power, norm, out):
    sums = jnp.sum(power * power, axis=0, keepdims=True)
    for i in range(16):
        norm[i : i + 1, :] = sums[:, i * 128 : i * 128 + 128]
    nb = norm[...].astype(BF)
    for i in range(16):
        out[i, R:, :] = nb


def refresh(blocks, power, norm, outs):
    sums = blocks[0, R:, :].astype(F32)
    for i in range(1, 16):
        sums = sums + blocks[i, R:, :].astype(F32)
    norm[...] = 1.0 / jnp.sqrt(sums / W + 1e-06)
    for i in range(16):
        cols = slice(i * R, (i + 1) * R)
        for k, out in enumerate(outs):
            out[C:R, cols] = (power[k * C : (k + 1) * C, cols] * norm[i : i + 1, :]).astype(BF)


def store_rows(pos, src, row, refs, sems, first):
    copies = []
    for k, off in enumerate(offsets(pos)):
        cp = pltpu.make_async_copy(src.at[pl.ds(pl.multiple_of(row + off, C), C), :], refs[k], sems.at[first + k])
        cp.start()
        copies.append(cp)
    return copies


def half_kernel(*args):
    pos, gs = args[0], args[1:3]
    out, power, basis, lhs, acc, norm, sems = args[-7:]
    rows = load_rows(pos, gs, ((0, 0), (1, R)), lhs, sems)
    groups = start_loads(pos, RIGHT, args[3:-7], basis, sems)
    for cp in rows:
        cp.wait()
    multiply(groups, lhs, basis, acc)
    stores = store_rows(pos, acc, R, (power.at[:C], power.at[C:]), sems, 40)
    for i in range(16):
        out[i, :R, :] = (acc[:R, i * R : (i + 1) * R] * ROOT).astype(BF)
    pack_sums(acc[R:, :], norm, out)
    for cp in stores:
        cp.wait()


def left_kernel(*args):
    pos, hcols = args[:2]
    gs, power_r = args[2:4], args[4]
    out, home0, home1, power, basis, lhs, acc, mom, dire, norm, right, sems = args[-12:]
    rows = load_rows(pos, gs, ((2, R),), lhs, sems)
    groups = start_loads(pos, LEFT, args[5:-12], basis, sems)
    later = load_rows(pos, gs, ((3, 0), (4, R)), mom, sems, 34)
    later.append(pltpu.make_async_copy(power_r, right, sems.at[42]))
    later[-1].start()
    for i in range(16):
        lhs[:R, i * R : (i + 1) * R] = hcols[i, :R, :].astype(F32).T.astype(BF)
    for cp in rows:
        cp.wait()
    multiply(groups, lhs, basis, acc)
    stores = store_rows(pos, acc, R, (power.at[:C], power.at[C:]), sems, 40)
    for cp in later:
        cp.wait()
    for i in range(16):
        cols = slice(i * R, (i + 1) * R)
        rot = acc[:R, cols] * ROOT
        nf = 0.9 * mom[:R, cols].astype(F32) + 0.1 * rot
        ns = 0.95 * mom[R:, cols].astype(F32) + 0.05 * rot * rot
        dire[cols, :] = (nf / (jnp.sqrt(ns) + 1e-8)).T.astype(BF)

    o0, o1 = offsets(pos)
    home0[:C, :] = (acc[pl.ds(o0, C), :] * ROOT).astype(BF)
    home1[:C, :] = (acc[pl.ds(o1, C), :] * ROOT).astype(BF)
    refresh(hcols, right, norm, (home0, home1))
    pack_sums(acc[R:, :], norm, out)

    @pl.loop(0, 2)
    def _(n):
        ro = pl.multiple_of(n * 1024, 1024)
        bk = (jnp.dot(basis[pl.ds(ro, 1024), :], dire[...], preferred_element_type=F32) * ROOT).astype(BF)
        for i in range(8):
            out[8 * n + i, :R, :] = bk[i * R : (i + 1) * R]

    for cp in stores:
        cp.wait()


def raw_kernel(*args):
    pos, brows, power_l = args[:3]
    home0, home1, total, basis, lhs, raw, left, norm, sems = args[-9:]
    groups = start_loads(pos, RIGHT, args[3:-9], basis, sems)
    power = pltpu.make_async_copy(power_l, left, sems.at[42])
    power.start()
    for i in range(16):
        lhs[:, i * R : (i + 1) * R] = brows[i, :R, :]
    tot = jnp.zeros((1, X), F32)
    for xoff, copies in groups:
        for cp in copies:
            cp.wait()
        r = lax.dot_general(
            lhs[...], basis[pl.ds(xoff, X), :], (((1,), (1,)), ((), ())), preferred_element_type=F32
        ) * ROOT
        tot = tot + jnp.sum(r * r, axis=0, keepdims=True)
        raw[:, pl.ds(xoff, X)] = r.astype(BF)
    o0, o1 = offsets(pos)
    home0[:C, :] = raw[pl.ds(o0, C), :]
    home1[:C, :] = raw[pl.ds(o1, C), :]
    power.wait()
    refresh(brows, left, norm, (home0, home1))
    total[...] = jnp.broadcast_to(jnp.sum(tot, axis=1, keepdims=True), (256, 128))


def sds(shape, dtype):
    return jax.ShapeDtypeStruct(shape, dtype)


def call(kernel, name, outs, in_hbm, scratch, flops, vmem_args, any_args):
    return pl.pallas_call(
        kernel,
        out_shape=outs,
        in_specs=[INS] + [INV] * (len(vmem_args) - 1) + [HBM] * len(any_args),
        out_specs=(INV,) * (len(outs) - in_hbm) + (HBM,) * in_hbm,
        scratch_shapes=scratch,
        compiler_params=pltpu.CompilerParams(vmem_limit_bytes=VMEM),
        cost_estimate=pl.CostEstimate(flops=flops, bytes_accessed=3 * W * W, transcendentals=0),
        name=name,
    )(*vmem_args, *any_args)


BASIS = pltpu.VMEM((W, W), BF)
SEMS = pltpu.SemaphoreType.DMA((43,))
NORM = pltpu.VMEM((16, 128), F32)
POWER = pltpu.VMEM((R, W), F32)
WIDE = pltpu.VMEM((2 * R, W), BF)
HOME = sds((R, W), BF)
BLOCKS = sds((16, R + 16, R), BF)


def call_half(pos, gs, pieces):
    scratch = [BASIS, WIDE, pltpu.VMEM((2 * R, W), F32), NORM, SEMS]
    outs = (BLOCKS, sds((R, W), F32))
    return call(half_kernel, "half", outs, 1, scratch, 4 * R * W * W, (pos,), (*gs, *pieces))


def call_left(pos, gs, hcols, power_r, pieces):
    scratch = [BASIS, WIDE, pltpu.VMEM((2 * R, W), F32), WIDE, pltpu.VMEM((W, R), BF), NORM, POWER, SEMS]
    outs = (BLOCKS, HOME, HOME, sds((R, W), F32))
    hbm_args = (*gs, power_r, *pieces)
    return call(left_kernel, "left", outs, 1, scratch, 6 * R * W * W, (pos, hcols), hbm_args)


def call_raw(pos, brows, power_l, pieces):
    scratch = [BASIS, pltpu.VMEM((R, W), BF), pltpu.VMEM((R, W), BF), POWER, NORM, SEMS]
    outs = (HOME, HOME, sds((256, 128), F32))
    return call(raw_kernel, "raw", outs, 0, scratch, 2 * R * W * W, (pos, brows), (power_l, *pieces))


def shift(v, by):
    return lax.ppermute(v, "x", [(i, (i + by) % 4) for i in range(4)])


def neighbours(block):
    return [shift(block, 1), shift(block, -1)]


def swap(v, axis):
    return lax.ppermute(v, axis, [(0, 1), (1, 0)])


def other_core(*blocks):
    return [swap(v, "c") for v in blocks]


def route(k):
    return [(c * 4 + 2 * h + b, h * 4 + 2 * c + (k ^ b)) for c in range(2) for h in range(2) for b in range(2)]


def there(v, k):
    return lax.ppermute(v, ("c", "y"), route(k))


def home(v, k):
    return lax.ppermute(v, ("c", "y"), [(b, a) for a, b in route(k)])


def after(v, *others):
    return lax.optimization_barrier((v,) + others)[0]


def body(grads, left_basis, right_basis, left_stat, right_stat, first_moment, second_moment, refresh_flags):
    c, x, zl, y = (lax.axis_index(a) for a in ("c", "x", "zl", "y"))
    pos = jnp.stack([c, x, zl, y]).astype(jnp.int32)
    odd = jnp.bitwise_and(y, 1)
    even = odd == 0

    def pick(a, k):
        return lax.dynamic_index_in_dim(a, jnp.bitwise_xor(odd, k), 0, keepdims=False)

    def send(*arrays):
        return [there(jnp.concatenate([pick(a, k) for a in arrays], axis=0), k) for k in range(2)]

    def collect(v0, v1):
        return jnp.where(even, jnp.stack([v0, v1]), jnp.stack([v1, v0]))

    firsts, seconds = (jnp.swapaxes(m, 1, 2) for m in (first_moment, second_moment))
    u, v = send(right_basis, left_basis)
    rest = send(after(grads, u, v), right_stat, left_stat, firsts.astype(BF), seconds.astype(BF))

    v_near = neighbours(v)
    uz = swap(u, "zl")
    u_near = neighbours(u)
    vz = swap(v, "zl")
    v_far = [shift(after(v_near[0][:C], uz), 1), shift(after(v_near[1][C:], uz), -1)]
    uz_near = neighbours(uz)
    v_all = jnp.concatenate([after(v_near[0], *u_near, vz, *rest), v_near[1], *v_far], axis=0)
    v_all_z = swap(v_all, "zl")
    far = [shift(after(u_near[0], *uz_near), 1), shift(after(uz_near[1], u_near[0]), -1)]
    pieces = [u, uz, *u_near, *uz_near, *far, v, vz, v_all, v_all_z]
    pieces += other_core(*pieces[:-1], after(v_all_z, *far))

    group = ("x", "zl", "c")
    half, power_r = call_half(pos, rest, pieces)
    hcols = lax.all_to_all(half, group, split_axis=0, concat_axis=0, tiled=True)
    back, home0, home1, power_l = call_left(pos, rest, hcols, power_r, pieces)
    brows = lax.all_to_all(back, group, split_axis=0, concat_axis=0, tiled=True)
    early = collect(home(after(home0, brows), 0), home(after(home1, brows), 1))
    home0, home1, total = call_raw(pos, brows, power_l, pieces)
    totals = lax.all_to_all(total, ("zh", "c", "x", "zl", "y"), split_axis=0, concat_axis=0, tiled=True)
    late = collect(home(home0, 0), home(home1, 1))

    def refreshed(side, part, basis):
        return jnp.where(refresh_flags[:, side, None, :] == 1, part, basis)

    new_left = refreshed(0, late[:, C:], left_basis)
    rotated = early[:, :C].astype(F32)
    new_right = refreshed(1, early[:, C:], right_basis)
    new_first = jnp.swapaxes(0.9 * firsts + 0.1 * rotated, 1, 2)
    new_second = jnp.swapaxes(0.95 * seconds + 0.05 * rotated * rotated, 1, 2)

    totals = after(totals, new_left, new_right, new_first, new_second)
    count = lax.axis_size(("zh", "c")) * 2 * W * W
    rms = jnp.sqrt(jnp.sum(totals[:, 0]) / count + 1e-06)
    factor = jnp.minimum(1.0, 0.5 / rms)
    update = (late[:, :C].astype(F32) * factor).astype(BF)
    return update, new_first, new_second, new_left, new_right


def solution(mesh):
    fine = Mesh(mesh.devices.reshape(4, 2, 4, 2, 4), ("zh", "c", "x", "zl", "y"))
    layer, fsdp = ("zh", "c"), ("x", "zl", "y")
    rows, cols = P(layer, fsdp, None), P(layer, None, fsdp)
    return jax.shard_map(
        body,
        mesh=fine,
        in_specs=(rows,) * 5 + (cols,) * 2 + (P(layer, None, None),),
        out_specs=(rows, cols, cols, rows, rows),
        check_vma=False,
    )
```

```python
import math

import jax
import jax.numpy as jnp
from jax import lax
from jax.experimental import pallas as pl
from jax.experimental.pallas import tpu as pltpu
from jax.sharding import Mesh, PartitionSpec as P

BF = jnp.bfloat16
F32 = jnp.float32
W = 2048
C = 64
R = 128
X = 512
ROOT = 1.0 / math.sqrt(W)
VMEM = 56 * 1024 * 1024
HBM = pl.BlockSpec(memory_space=pltpu.HBM)
INV = pl.BlockSpec(memory_space=pltpu.VMEM)
INS = pl.BlockSpec(memory_space=pltpu.SMEM)


def buffer_list():
    out = []
    for v, blocks in ((0, ((0, 0), (0, 1), (-1, 0), (1, 0), (-1, 1), (1, 1), (2, 0), (2, 1))), (1, ((0, 0), (0, 1)))):
        for dx, dz in blocks:
            out.append(([(0, dx, dz, v)], [(C, dx, dz, v)]))
    for dz in range(2):
        out.append(([(0, -1, dz, 1), (2 * C, 1, dz, 1), (4 * C, 2, dz, 1)], [(C, -1, dz, 1), (3 * C, 1, dz, 1), (5 * C, 2, dz, 1)]))
    return out


BUFFERS = buffer_list()
RIGHT, LEFT = 0, 1


def start_loads(pos, side, refs, dst, sems):
    c, x, zl = pos[0], pos[1], pos[2]
    places = offsets(pos)
    groups = []
    n = 0
    for step in (0, -1, 1, 2):
        xoff = pl.multiple_of(jnp.bitwise_and(x + step + 4, 3) * X, X)
        copies = []
        for dc in range(2):
            for buf, parts in enumerate(BUFFERS):
                for row, dx, dz, which in parts[side]:
                    if dx != step:
                        continue
                    z = jnp.bitwise_and(zl + dz, 1)
                    cc = jnp.bitwise_and(c + dc, 1)
                    off = pl.multiple_of(xoff + z * (2 * R) + cc * R + places[which], C)
                    cp = pltpu.make_async_copy(
                        refs[dc * len(BUFFERS) + buf].at[pl.ds(row, C), :],
                        dst.at[pl.ds(off, C), :],
                        sems.at[n],
                    )
                    cp.start()
                    copies.append(cp)
                    n += 1
        groups.append((xoff, copies))
    return groups


def offsets(pos):
    odd = jnp.bitwise_and(pos[3], 1)
    return pl.multiple_of(odd * C, C), pl.multiple_of((1 - odd) * C, C)


def load_rows(pos, refs, parts, dst, sems, first=32):
    copies = []
    for k, off in enumerate(offsets(pos)):
        for part, row in parts:
            cp = pltpu.make_async_copy(
                refs[k].at[pl.ds(part * C, C), :],
                dst.at[pl.ds(pl.multiple_of(row + off, C), C), :],
                sems.at[first + len(copies)],
            )
            cp.start()
            copies.append(cp)
    return copies


def multiply(groups, lhs, basis, acc):
    for i, (xoff, copies) in enumerate(groups):
        for cp in copies:
            cp.wait()

        part = jnp.dot(lhs[:, pl.ds(xoff, X)], basis[pl.ds(xoff, X), :], preferred_element_type=F32)
        if i == 0:
            acc[...] = part
        else:
            acc[...] += part


def pack_sums(power, norm, out):
    sums = jnp.sum(power * power, axis=0, keepdims=True)
    for i in range(16):
        norm[i : i + 1, :] = sums[:, i * 128 : i * 128 + 128]
    nb = norm[...].astype(BF)
    for i in range(16):
        out[i, R:, :] = nb


def refresh(blocks, power, norm, outs):
    sums = blocks[0, R:, :].astype(F32)
    for i in range(1, 16):
        sums = sums + blocks[i, R:, :].astype(F32)
    norm[...] = 1.0 / jnp.sqrt(sums / W + 1e-06)
    for i in range(16):
        cols = slice(i * R, (i + 1) * R)
        for k, out in enumerate(outs):
            out[C:R, cols] = (power[k * C : (k + 1) * C, cols] * norm[i : i + 1, :]).astype(BF)


def store_rows(pos, src, row, refs, sems, first):
    copies = []
    for k, off in enumerate(offsets(pos)):
        cp = pltpu.make_async_copy(src.at[pl.ds(pl.multiple_of(row + off, C), C), :], refs[k], sems.at[first + k])
        cp.start()
        copies.append(cp)
    return copies


def half_kernel(*args):
    pos, gs = args[0], args[1:3]
    out, power, basis, lhs, acc, norm, sems = args[-7:]
    rows = load_rows(pos, gs, ((0, 0), (1, R)), lhs, sems)
    groups = start_loads(pos, RIGHT, args[3:-7], basis, sems)
    for cp in rows:
        cp.wait()
    multiply(groups, lhs, basis, acc)
    stores = store_rows(pos, acc, R, (power.at[:C], power.at[C:]), sems, 40)
    for i in range(16):
        out[i, :R, :] = (acc[:R, i * R : (i + 1) * R] * ROOT).astype(BF)
    pack_sums(acc[R:, :], norm, out)
    for cp in stores:
        cp.wait()


def left_kernel(*args):
    pos, hcols = args[:2]
    gs, power_r = args[2:4], args[4]
    out, home0, home1, power, basis, lhs, acc, mom, dire, norm, right, sems = args[-12:]
    rows = load_rows(pos, gs, ((2, R),), lhs, sems)
    rows.append(pltpu.make_async_copy(power_r, right, sems.at[42]))
    rows[-1].start()
    groups = start_loads(pos, LEFT, args[5:-12], basis, sems)
    later = load_rows(pos, gs, ((3, 0), (4, R)), mom, sems, 34)
    for i in range(16):
        lhs[:R, i * R : (i + 1) * R] = hcols[i, :R, :].astype(F32).T.astype(BF)
    for cp in rows:
        cp.wait()
    refresh(hcols, right, norm, (home0, home1))
    multiply(groups, lhs, basis, acc)
    stores = store_rows(pos, acc, R, (power.at[:C], power.at[C:]), sems, 40)
    for cp in later:
        cp.wait()
    for i in range(16):
        cols = slice(i * R, (i + 1) * R)
        rot = acc[:R, cols] * ROOT
        nf = 0.9 * mom[:R, cols].astype(F32) + 0.1 * rot
        ns = 0.95 * mom[R:, cols].astype(F32) + 0.05 * rot * rot
        dire[cols, :] = (nf / (jnp.sqrt(ns) + 1e-8)).T.astype(BF)

    o0, o1 = offsets(pos)
    home0[:C, :] = (acc[pl.ds(o0, C), :] * ROOT).astype(BF)
    home1[:C, :] = (acc[pl.ds(o1, C), :] * ROOT).astype(BF)
    pack_sums(acc[R:, :], norm, out)

    @pl.loop(0, 2)
    def _(n):
        ro = pl.multiple_of(n * 1024, 1024)
        bk = (jnp.dot(basis[pl.ds(ro, 1024), :], dire[...], preferred_element_type=F32) * ROOT).astype(BF)
        for i in range(8):
            out[8 * n + i, :R, :] = bk[i * R : (i + 1) * R]

    for cp in stores:
        cp.wait()


def raw_kernel(*args):
    pos, brows, power_l = args[:3]
    home0, home1, total, basis, lhs, raw, left, norm, sems = args[-9:]
    power = pltpu.make_async_copy(power_l, left, sems.at[42])
    power.start()
    groups = start_loads(pos, RIGHT, args[3:-9], basis, sems)
    for i in range(16):
        lhs[:, i * R : (i + 1) * R] = brows[i, :R, :]
    power.wait()
    refresh(brows, left, norm, (home0, home1))
    tot = jnp.zeros((1, X), F32)
    for xoff, copies in groups:
        for cp in copies:
            cp.wait()
        r = lax.dot_general(
            lhs[...], basis[pl.ds(xoff, X), :], (((1,), (1,)), ((), ())), preferred_element_type=F32
        ) * ROOT
        tot = tot + jnp.sum(r * r, axis=0, keepdims=True)
        raw[:, pl.ds(xoff, X)] = r.astype(BF)
    o0, o1 = offsets(pos)
    home0[:C, :] = raw[pl.ds(o0, C), :]
    home1[:C, :] = raw[pl.ds(o1, C), :]
    total[...] = jnp.broadcast_to(jnp.sum(tot, axis=1, keepdims=True), (256, 128))


def sds(shape, dtype):
    return jax.ShapeDtypeStruct(shape, dtype)


def call(kernel, name, outs, in_hbm, scratch, flops, vmem_args, any_args):
    return pl.pallas_call(
        kernel,
        out_shape=outs,
        in_specs=[INS] + [INV] * (len(vmem_args) - 1) + [HBM] * len(any_args),
        out_specs=(INV,) * (len(outs) - in_hbm) + (HBM,) * in_hbm,
        scratch_shapes=scratch,
        compiler_params=pltpu.CompilerParams(vmem_limit_bytes=VMEM),
        cost_estimate=pl.CostEstimate(flops=flops, bytes_accessed=3 * W * W, transcendentals=0),
        name=name,
    )(*vmem_args, *any_args)


BASIS = pltpu.VMEM((W, W), BF)
SEMS = pltpu.SemaphoreType.DMA((43,))
NORM = pltpu.VMEM((16, 128), F32)
POWER = pltpu.VMEM((R, W), F32)
WIDE = pltpu.VMEM((2 * R, W), BF)
HOME = sds((R, W), BF)
BLOCKS = sds((16, R + 16, R), BF)


def call_half(pos, gs, pieces):
    scratch = [BASIS, WIDE, pltpu.VMEM((2 * R, W), F32), NORM, SEMS]
    outs = (BLOCKS, sds((R, W), F32))
    return call(half_kernel, "half", outs, 1, scratch, 4 * R * W * W, (pos,), (*gs, *pieces))


def call_left(pos, gs, hcols, power_r, pieces):
    scratch = [BASIS, WIDE, pltpu.VMEM((2 * R, W), F32), WIDE, pltpu.VMEM((W, R), BF), NORM, POWER, SEMS]
    outs = (BLOCKS, HOME, HOME, sds((R, W), F32))
    hbm_args = (*gs, power_r, *pieces)
    return call(left_kernel, "left", outs, 1, scratch, 6 * R * W * W, (pos, hcols), hbm_args)


def call_raw(pos, brows, power_l, pieces):
    scratch = [BASIS, pltpu.VMEM((R, W), BF), pltpu.VMEM((R, W), BF), POWER, NORM, SEMS]
    outs = (HOME, HOME, sds((256, 128), F32))
    return call(raw_kernel, "raw", outs, 0, scratch, 2 * R * W * W, (pos, brows), (power_l, *pieces))


def shift(v, by):
    return lax.ppermute(v, "x", [(i, (i + by) % 4) for i in range(4)])


def neighbours(block):
    return [shift(block, 1), shift(block, -1)]


def swap(v, axis):
    return lax.ppermute(v, axis, [(0, 1), (1, 0)])


def other_core(*blocks):
    return [swap(v, "c") for v in blocks]


def route(k):
    return [(c * 4 + 2 * h + b, h * 4 + 2 * c + (k ^ b)) for c in range(2) for h in range(2) for b in range(2)]


def there(v, k):
    return lax.ppermute(v, ("c", "y"), route(k))


def home(v, k):
    return lax.ppermute(v, ("c", "y"), [(b, a) for a, b in route(k)])


def after(v, *others):
    return lax.optimization_barrier((v,) + others)[0]


def body(grads, left_basis, right_basis, left_stat, right_stat, first_moment, second_moment, refresh_flags):
    c, x, zl, y = (lax.axis_index(a) for a in ("c", "x", "zl", "y"))
    pos = jnp.stack([c, x, zl, y]).astype(jnp.int32)
    odd = jnp.bitwise_and(y, 1)
    even = odd == 0

    def pick(a, k):
        return lax.dynamic_index_in_dim(a, jnp.bitwise_xor(odd, k), 0, keepdims=False)

    def send(*arrays):
        return [there(jnp.concatenate([pick(a, k) for a in arrays], axis=0), k) for k in range(2)]

    def collect(v0, v1):
        return jnp.where(even, jnp.stack([v0, v1]), jnp.stack([v1, v0]))

    firsts, seconds = (jnp.swapaxes(m, 1, 2) for m in (first_moment, second_moment))
    u, v = send(right_basis, left_basis)
    rest = send(after(grads, u, v), right_stat, left_stat, firsts.astype(BF), seconds.astype(BF))

    v_near = neighbours(v)
    uz = swap(u, "zl")
    u_near = neighbours(u)
    vz = swap(v, "zl")
    v_far = [shift(after(v_near[0][:C], uz), 1), shift(after(v_near[1][C:], uz), -1)]
    uz_near = neighbours(uz)
    v_all = jnp.concatenate([after(v_near[0], *u_near, vz, *rest), v_near[1], *v_far], axis=0)
    v_all_z = swap(v_all, "zl")
    far = [shift(after(u_near[0], *uz_near), 1), shift(after(uz_near[1], u_near[0]), -1)]
    pieces = [u, uz, *u_near, *uz_near, *far, v, vz, v_all, v_all_z]
    c_early = other_core(u, uz, *u_near)
    c_late = other_core(*uz_near, *far)
    v_early = other_core(v, vz)
    pieces += c_early + c_late + v_early + other_core(v_all, after(v_all_z, *far, *c_early, *v_early))

    group = ("x", "zl", "c")
    half, power_r = call_half(pos, rest, pieces)
    hcols = lax.all_to_all(half, group, split_axis=0, concat_axis=0, tiled=True)
    back, home0, home1, power_l = call_left(pos, rest, hcols, power_r, pieces)
    brows = lax.all_to_all(back, group, split_axis=0, concat_axis=0, tiled=True)
    early = collect(home(after(home0, brows), 0), home(after(home1, brows), 1))
    home0, home1, total = call_raw(pos, brows, power_l, pieces)
    totals = lax.all_to_all(total, ("zh", "c", "x", "zl", "y"), split_axis=0, concat_axis=0, tiled=True)
    late = collect(home(home0, 0), home(home1, 1))

    def refreshed(side, part, basis):
        return jnp.where(refresh_flags[:, side, None, :] == 1, part, basis)

    new_left = refreshed(0, late[:, C:], left_basis)
    rotated = early[:, :C].astype(F32)
    new_right = refreshed(1, early[:, C:], right_basis)
    new_first = jnp.swapaxes(0.9 * firsts + 0.1 * rotated, 1, 2)
    new_second = jnp.swapaxes(0.95 * seconds + 0.05 * rotated * rotated, 1, 2)

    totals = after(totals, new_left, new_right, new_first, new_second)
    count = lax.axis_size(("zh", "c")) * 2 * W * W
    rms = jnp.sqrt(jnp.sum(totals[:, 0]) / count + 1e-06)
    factor = jnp.minimum(1.0, 0.5 / rms)
    update = (late[:, :C].astype(F32) * factor).astype(BF)
    return update, new_first, new_second, new_left, new_right


def solution(mesh):
    fine = Mesh(mesh.devices.reshape(4, 2, 4, 2, 4), ("zh", "c", "x", "zl", "y"))
    layer, fsdp = ("zh", "c"), ("x", "zl", "y")
    rows, cols = P(layer, fsdp, None), P(layer, None, fsdp)
    return jax.shard_map(
        body,
        mesh=fine,
        in_specs=(rows,) * 5 + (cols,) * 2 + (P(layer, None, None),),
        out_specs=(rows, cols, cols, rows, rows),
        check_vma=False,
    )
```

```python
import math

import jax
import jax.numpy as jnp
from jax import lax
from jax.experimental import pallas as pl
from jax.experimental.pallas import tpu as pltpu
from jax.sharding import Mesh, PartitionSpec as P

BF = jnp.bfloat16
F32 = jnp.float32
W = 2048
C = 64
R = 128
X = 512
ROOT = 1.0 / math.sqrt(W)
VMEM = 60 * 1024 * 1024
HBM = pl.BlockSpec(memory_space=pltpu.HBM)
INV = pl.BlockSpec(memory_space=pltpu.VMEM)
INS = pl.BlockSpec(memory_space=pltpu.SMEM)


def buffer_list():
    out = []
    for v, blocks in ((0, ((0, 0), (0, 1), (-1, 0), (1, 0), (-1, 1), (1, 1), (2, 0), (2, 1))), (1, ((0, 0), (0, 1)))):
        for dx, dz in blocks:
            out.append(([(0, dx, dz, v)], [(C, dx, dz, v)]))
    for dz in range(2):
        out.append(([(0, -1, dz, 1), (2 * C, 1, dz, 1), (4 * C, 2, dz, 1)], [(C, -1, dz, 1), (3 * C, 1, dz, 1), (5 * C, 2, dz, 1)]))
    return out


BUFFERS = buffer_list()
RIGHT, LEFT = 0, 1


def start_loads(pos, side, refs, dst, sems):
    c, x, zl = pos[0], pos[1], pos[2]
    places = offsets(pos)
    groups = []
    n = 0
    for step in (0, -1, 1, 2):
        xoff = pl.multiple_of(jnp.bitwise_and(x + step + 4, 3) * X, X)
        copies = []
        for dc in range(2):
            for buf, parts in enumerate(BUFFERS):
                for row, dx, dz, which in parts[side]:
                    if dx != step:
                        continue
                    z = jnp.bitwise_and(zl + dz, 1)
                    cc = jnp.bitwise_and(c + dc, 1)
                    off = pl.multiple_of(xoff + z * (2 * R) + cc * R + places[which], C)
                    cp = pltpu.make_async_copy(
                        refs[dc * len(BUFFERS) + buf].at[pl.ds(row, C), :],
                        dst.at[pl.ds(off, C), :],
                        sems.at[n],
                    )
                    cp.start()
                    copies.append(cp)
                    n += 1
        groups.append((xoff, copies))
    return groups


def offsets(pos):
    odd = jnp.bitwise_and(pos[3], 1)
    return pl.multiple_of(odd * C, C), pl.multiple_of((1 - odd) * C, C)


def load_rows(pos, refs, parts, dst, sems, first=32):
    copies = []
    for k, off in enumerate(offsets(pos)):
        for part, row in parts:
            cp = pltpu.make_async_copy(
                refs[k].at[pl.ds(part * C, C), :],
                dst.at[pl.ds(pl.multiple_of(row + off, C), C), :],
                sems.at[first + len(copies)],
            )
            cp.start()
            copies.append(cp)
    return copies


def multiply(groups, lhs, basis, acc):
    for i, (xoff, copies) in enumerate(groups):
        for cp in copies:
            cp.wait()

        part = jnp.dot(lhs[:, pl.ds(xoff, X)], basis[pl.ds(xoff, X), :], preferred_element_type=F32)
        if i == 0:
            acc[...] = part
        else:
            acc[...] += part


def pack_sums(power, norm, out):
    sums = jnp.sum(power * power, axis=0, keepdims=True)
    for i in range(16):
        norm[i : i + 1, :] = sums[:, i * 128 : i * 128 + 128]
    nb = norm[...].astype(BF)
    for i in range(16):
        out[i, R:, :] = nb


def refresh(blocks, power, norm, outs):
    sums = blocks[0, R:, :].astype(F32)
    for i in range(1, 16):
        sums = sums + blocks[i, R:, :].astype(F32)
    norm[...] = 1.0 / jnp.sqrt(sums / W + 1e-06)
    for i in range(16):
        cols = slice(i * R, (i + 1) * R)
        for k, out in enumerate(outs):
            out[C:R, cols] = (power[k * C : (k + 1) * C, cols] * norm[i : i + 1, :]).astype(BF)


def store_rows(pos, src, row, refs, sems, first):
    copies = []
    for k, off in enumerate(offsets(pos)):
        cp = pltpu.make_async_copy(src.at[pl.ds(pl.multiple_of(row + off, C), C), :], refs[k], sems.at[first + k])
        cp.start()
        copies.append(cp)
    return copies


def half_kernel(*args):
    pos, gs = args[0], args[1:3]
    out, power, basis, lhs, acc, norm, sems = args[-7:]
    rows = load_rows(pos, gs, ((0, 0), (1, R)), lhs, sems)
    groups = start_loads(pos, RIGHT, args[3:-7], basis, sems)
    for cp in rows:
        cp.wait()
    multiply(groups, lhs, basis, acc)
    stores = store_rows(pos, acc, R, (power.at[:C], power.at[C:]), sems, 40)
    for i in range(16):
        out[i, :R, :] = (acc[:R, i * R : (i + 1) * R] * ROOT).astype(BF)
    pack_sums(acc[R:, :], norm, out)
    for cp in stores:
        cp.wait()


def left_kernel(*args):
    pos, hcols = args[:2]
    gs, power_r = args[2:4], args[4]
    out, home0, home1, power, basis, lhs, acc, mom, dire, norm, right, sems = args[-12:]
    rows = load_rows(pos, gs, ((2, R),), lhs, sems)
    rows.append(pltpu.make_async_copy(power_r, right, sems.at[42]))
    rows[-1].start()
    groups = start_loads(pos, LEFT, args[5:-12], basis, sems)
    later = load_rows(pos, gs, ((3, 0), (4, R)), mom, sems, 34)
    for i in range(16):
        lhs[:R, i * R : (i + 1) * R] = hcols[i, :R, :].astype(F32).T.astype(BF)
    for cp in rows:
        cp.wait()
    refresh(hcols, right, norm, (home0, home1))
    multiply(groups, lhs, basis, acc)
    stores = store_rows(pos, acc, R, (power.at[:C], power.at[C:]), sems, 40)
    for cp in later:
        cp.wait()
    for i in range(16):
        cols = slice(i * R, (i + 1) * R)
        rot = acc[:R, cols] * ROOT
        nf = 0.9 * mom[:R, cols].astype(F32) + 0.1 * rot
        ns = 0.95 * mom[R:, cols].astype(F32) + 0.05 * rot * rot
        dire[cols, :] = (nf / (jnp.sqrt(ns) + 1e-8)).T.astype(BF)

    o0, o1 = offsets(pos)
    home0[:C, :] = (acc[pl.ds(o0, C), :] * ROOT).astype(BF)
    home1[:C, :] = (acc[pl.ds(o1, C), :] * ROOT).astype(BF)
    pack_sums(acc[R:, :], norm, out)

    @pl.loop(0, 2)
    def _(n):
        ro = pl.multiple_of(n * 1024, 1024)
        bk = (jnp.dot(basis[pl.ds(ro, 1024), :], dire[...], preferred_element_type=F32) * ROOT).astype(BF)
        for i in range(8):
            out[8 * n + i, :R, :] = bk[i * R : (i + 1) * R]

    for cp in stores:
        cp.wait()


def raw_kernel(*args):
    pos, brows, power_l = args[:3]
    home0, home1, total, basis, lhs, raw, left, norm, sems = args[-9:]
    power = pltpu.make_async_copy(power_l, left, sems.at[42])
    power.start()
    groups = start_loads(pos, RIGHT, args[3:-9], basis, sems)
    for i in range(16):
        lhs[:, i * R : (i + 1) * R] = brows[i, :R, :]
    power.wait()
    refresh(brows, left, norm, (home0, home1))
    tot = jnp.zeros((1, X), F32)
    for xoff, copies in groups:
        for cp in copies:
            cp.wait()
        r = lax.dot_general(
            lhs[...], basis[pl.ds(xoff, X), :], (((1,), (1,)), ((), ())), preferred_element_type=F32
        ) * ROOT
        tot = tot + jnp.sum(r * r, axis=0, keepdims=True)
        raw[:, pl.ds(xoff, X)] = r.astype(BF)
    o0, o1 = offsets(pos)
    home0[:C, :] = raw[pl.ds(o0, C), :]
    home1[:C, :] = raw[pl.ds(o1, C), :]
    total[...] = jnp.broadcast_to(jnp.sum(tot, axis=1, keepdims=True), (256, 128))


def sds(shape, dtype):
    return jax.ShapeDtypeStruct(shape, dtype)


def call(kernel, name, outs, in_hbm, scratch, flops, vmem_args, any_args):
    return pl.pallas_call(
        kernel,
        out_shape=outs,
        in_specs=[INS] + [INV] * (len(vmem_args) - 1) + [HBM] * len(any_args),
        out_specs=(INV,) * (len(outs) - in_hbm) + (HBM,) * in_hbm,
        scratch_shapes=scratch,
        compiler_params=pltpu.CompilerParams(vmem_limit_bytes=VMEM),
        cost_estimate=pl.CostEstimate(flops=flops, bytes_accessed=3 * W * W, transcendentals=0),
        name=name,
    )(*vmem_args, *any_args)


BASIS = pltpu.VMEM((W, W), BF)
SEMS = pltpu.SemaphoreType.DMA((43,))
NORM = pltpu.VMEM((16, 128), F32)
POWER = pltpu.VMEM((R, W), F32)
WIDE = pltpu.VMEM((2 * R, W), BF)
HOME = sds((R, W), BF)
BLOCKS = sds((16, R + 16, R), BF)


def call_half(pos, gs, pieces):
    scratch = [BASIS, WIDE, pltpu.VMEM((2 * R, W), F32), NORM, SEMS]
    outs = (BLOCKS, sds((R, W), F32))
    return call(half_kernel, "half", outs, 1, scratch, 4 * R * W * W, (pos,), (*gs, *pieces))


def call_left(pos, gs, hcols, power_r, pieces):
    scratch = [BASIS, WIDE, pltpu.VMEM((2 * R, W), F32), WIDE, pltpu.VMEM((W, R), BF), NORM, POWER, SEMS]
    outs = (BLOCKS, HOME, HOME, sds((R, W), F32))
    hbm_args = (*gs, power_r, *pieces)
    return call(left_kernel, "left", outs, 1, scratch, 6 * R * W * W, (pos, hcols), hbm_args)


def call_raw(pos, brows, power_l, pieces):
    scratch = [BASIS, pltpu.VMEM((R, W), BF), pltpu.VMEM((R, W), BF), POWER, NORM, SEMS]
    outs = (HOME, HOME, sds((256, 128), F32))
    return call(raw_kernel, "raw", outs, 0, scratch, 2 * R * W * W, (pos, brows), (power_l, *pieces))


def shift(v, by):
    return lax.ppermute(v, "x", [(i, (i + by) % 4) for i in range(4)])


def neighbours(block):
    return [shift(block, 1), shift(block, -1)]


def swap(v, axis):
    return lax.ppermute(v, axis, [(0, 1), (1, 0)])


def other_core(*blocks):
    return [swap(v, "c") for v in blocks]


def route(k):
    return [(c * 4 + 2 * h + b, h * 4 + 2 * c + (k ^ b)) for c in range(2) for h in range(2) for b in range(2)]


def there(v, k):
    return lax.ppermute(v, ("c", "y"), route(k))


def home(v, k):
    return lax.ppermute(v, ("c", "y"), [(b, a) for a, b in route(k)])


def after(v, *others):
    return lax.optimization_barrier((v,) + others)[0]


def body(grads, left_basis, right_basis, left_stat, right_stat, first_moment, second_moment, refresh_flags):
    c, x, zl, y = (lax.axis_index(a) for a in ("c", "x", "zl", "y"))
    pos = jnp.stack([c, x, zl, y]).astype(jnp.int32)
    odd = jnp.bitwise_and(y, 1)
    even = odd == 0

    def pick(a, k):
        return lax.dynamic_index_in_dim(a, jnp.bitwise_xor(odd, k), 0, keepdims=False)

    def send(*arrays):
        return [there(jnp.concatenate([pick(a, k) for a in arrays], axis=0), k) for k in range(2)]

    def collect(v0, v1):
        return jnp.where(even, jnp.stack([v0, v1]), jnp.stack([v1, v0]))

    firsts, seconds = (jnp.swapaxes(m, 1, 2) for m in (first_moment, second_moment))
    u, v = send(right_basis, left_basis)
    rest = send(after(grads, u, v), right_stat, left_stat, firsts.astype(BF), seconds.astype(BF))

    v_near = neighbours(v)
    uz = swap(u, "zl")
    u_near = neighbours(u)
    vz = swap(v, "zl")
    v_far = [shift(after(v_near[0][:C], uz), 1), shift(after(v_near[1][C:], uz), -1)]
    uz_near = neighbours(uz)
    v_all = jnp.concatenate([after(v_near[0], *u_near, vz, *rest), v_near[1], *v_far], axis=0)
    v_all_z = swap(v_all, "zl")
    far = [shift(after(u_near[0], *uz_near), 1), shift(after(uz_near[1], u_near[0]), -1)]
    pieces = [u, uz, *u_near, *uz_near, *far, v, vz, v_all, v_all_z]
    c_early = other_core(u, uz, *u_near)
    c_late = other_core(*uz_near, *far)
    v_early = other_core(v, vz)
    pieces += c_early + c_late + v_early + other_core(v_all, after(v_all_z, *far, *c_early, *v_early))

    group = ("x", "zl", "c")
    half, power_r = call_half(pos, rest, pieces)
    hcols = lax.all_to_all(half, group, split_axis=0, concat_axis=0, tiled=True)
    back, home0, home1, power_l = call_left(pos, rest, hcols, power_r, pieces)
    brows = lax.all_to_all(back, group, split_axis=0, concat_axis=0, tiled=True)
    early = collect(home(after(home0, brows), 0), home(after(home1, brows), 1))
    home0, home1, total = call_raw(pos, brows, power_l, pieces)
    totals = lax.all_to_all(total, ("zh", "c", "x", "zl", "y"), split_axis=0, concat_axis=0, tiled=True)
    late = collect(home(home0, 0), home(home1, 1))

    def refreshed(side, part, basis):
        return jnp.where(refresh_flags[:, side, None, :] == 1, part, basis)

    new_left = refreshed(0, late[:, C:], left_basis)
    rotated = early[:, :C].astype(F32)
    new_right = refreshed(1, early[:, C:], right_basis)
    new_first = jnp.swapaxes(0.9 * firsts + 0.1 * rotated, 1, 2)
    new_second = jnp.swapaxes(0.95 * seconds + 0.05 * rotated * rotated, 1, 2)

    totals = after(totals, new_left, new_right, new_first, new_second)
    count = lax.axis_size(("zh", "c")) * 2 * W * W
    rms = jnp.sqrt(jnp.sum(totals[:, 0]) / count + 1e-06)
    factor = jnp.minimum(1.0, 0.5 / rms)
    update = (late[:, :C].astype(F32) * factor).astype(BF)
    return update, new_first, new_second, new_left, new_right


def solution(mesh):
    fine = Mesh(mesh.devices.reshape(4, 2, 4, 2, 4), ("zh", "c", "x", "zl", "y"))
    layer, fsdp = ("zh", "c"), ("x", "zl", "y")
    rows, cols = P(layer, fsdp, None), P(layer, None, fsdp)
    return jax.shard_map(
        body,
        mesh=fine,
        in_specs=(rows,) * 5 + (cols,) * 2 + (P(layer, None, None),),
        out_specs=(rows, cols, cols, rows, rows),
        check_vma=False,
    )
```
